512 devices in a mesh: dp: 32 (over x_lo, z, core), tensor: 16 (over y, x_hi).
Axes of the slice: x: 4 (x_hi: 2, x_lo: 2; x = x_hi * 2 + x_lo), y: 8, z: 8, core: 2. Of those that a mesh axis runs over, the one named last changes fastest.
Arguments:
- teacher_hidden: bfloat16 [65536, 8192], P('dp', 'tensor'), may hold values from -6 to 6
- teacher_gain: bfloat16 [8192], P('tensor'), may hold values from 0.5 to 1.5
- student_hidden: bfloat16 [65536, 2048], P(('dp', 'tensor')), may hold values from -6 to 6
- student_gain: float32 [2048], replicated, may hold values from 0.5 to 1.5
- projection: bfloat16 [2048, 8192], P('dp', 'tensor'), may hold values from -0.125 to 0.125
- lengths: int32 [32], P('dp'), may hold values from 1 to 2048, as said below
Outputs:
- loss: float32 [], replicated
- grad_gain: float32 [2048], replicated
- grad_proj: float32 [2048, 8192], P('dp', 'tensor')
The draws below stay inside these ranges and needn't reach their ends.
Inputs may be any that keep to these rules, and one draw needn't show every extreme that they name: `lengths`: one sequence has exactly 2048 valid positions.
All inputs are finite; a program needn't handle non-finite values.
Results may differ from the reference program's by a relative error of at most 0.002.
Values may be sent and summed in bfloat16 or wider, within the bound.
No kernel may reach another device: no remote copies, remote signals or barrier semaphores. Data moves between devices by JAX's collectives and lax.ppermute only.
A program may use at most 64 MiB of HBM per device.

```python
import jax
import jax.numpy as jnp
from jax import lax

SW = 2048
TW = 8192
LEN = 2048
SEQS = 32
TOKENS = 65536


def draw_lengths(key, part):
    key = jax.random.fold_in(key, 7)
    key_cap, key_each, key_full = jax.random.split(key, 3)
    ceiling = jax.random.randint(key_cap, (), LEN // 4, LEN + 1, dtype=jnp.int32)
    drawn = jax.random.randint(key_each, (SEQS,), 1, ceiling + 1, dtype=jnp.int32)
    chosen = jax.random.randint(key_full, (), 0, SEQS, dtype=jnp.int32)
    slots = jnp.arange(SEQS, dtype=jnp.int32)
    return jnp.where(slots == chosen, jnp.int32(LEN), drawn).astype(jnp.int32)


def level_of(own_key, dims, shards, low, high):
    gain, own = 1.0, jax.random.fold_in(own_key, 6)
    for dim, blocks in shards:
        heights = jnp.exp(jax.random.uniform(jax.random.fold_in(own, dim), (blocks,), jnp.float32, low / len(shards), high / len(shards)))
        gain = gain * jnp.repeat(heights, dims[dim] // blocks).reshape([-1 if axis == dim else 1 for axis in range(len(dims))])
    return gain


def normal_values(rng, shape, spread, limit, shards=(), held_as=jnp.bfloat16):
    gain = level_of(rng, shape, shards, -0.22, 0.18) if shards else 1.0
    array = jax.random.normal(rng, shape, jnp.float32) * spread * gain
    return jnp.minimum(jnp.maximum(array, -limit), limit).astype(held_as)


def setup_inputs(seed: int = 0) -> dict:
    key_of = jax.random.split(jax.random.key(seed), 7)
    return {
        "teacher_hidden": normal_values(key_of[0], (TOKENS, TW), 1.0, 6.0, ((0, 32), (1, 16))),
        "teacher_gain": jnp.clip(1.0 + 0.1 * jax.random.normal(key_of[1], (TW,), jnp.float32), 0.5, 1.5).astype(jnp.bfloat16),
        "student_hidden": normal_values(key_of[2], (TOKENS, SW), 1.0, 6.0, ((0, 512),)),
        "student_gain": jnp.clip(1.0 + 0.1 * jax.random.normal(key_of[3], (SW,), jnp.float32), 0.5, 1.5),
        "projection": normal_values(key_of[4], (SW, TW), SW ** -0.5, 0.125, ((0, 32), (1, 16))),
        "lengths": draw_lengths(jax.random.fold_in(key_of[6], 71), 0),
    }


epsilon = 1e-06

def reference(teacher_hidden, teacher_gain, student_hidden, student_gain, projection, lengths):
    student_f = student_hidden.astype(jnp.float32)
    normed = student_f * lax.rsqrt(lax.optimization_barrier(jnp.mean(student_f * student_f, axis=1, keepdims=True)) + epsilon)
    scaled = (normed * student_gain).astype(jnp.bfloat16)
    count = jnp.sum(lengths).astype(jnp.float32)
    gain_teacher = teacher_gain.astype(jnp.float32)
    teacher_seq = teacher_hidden.reshape(SEQS, LEN, TW)
    scaled_seq = scaled.reshape(SEQS, LEN, SW)

    def per_sequence(totals, inputs):
        grad_total, loss_total = totals
        teacher_rows, student_rows, length_here = inputs
        hidden_f = teacher_rows.astype(jnp.float32)
        target = hidden_f * lax.rsqrt(lax.optimization_barrier(jnp.mean(hidden_f * hidden_f, axis=1, keepdims=True)) + epsilon) * gain_teacher
        predicted = jnp.dot(student_rows, projection, preferred_element_type=jnp.float32)
        positions = jnp.arange(LEN, dtype=jnp.int32)
        valid = positions < length_here
        diff = jnp.where(valid[:, None], predicted - target, jnp.float32(0.0))
        slope = (diff * (2.0 / count)).astype(jnp.bfloat16)
        grad_total = grad_total + jnp.dot(student_rows.T, slope, preferred_element_type=jnp.float32)
        loss_total = loss_total + jnp.sum(diff * diff)
        return ((grad_total, loss_total), None)
    start_totals = (jnp.zeros((SW, TW), jnp.float32), jnp.zeros((), jnp.float32))
    (grad_proj, loss_sum), unused = lax.scan(per_sequence, start_totals, (teacher_seq, scaled_seq, lengths))
    loss = loss_sum / (count * TW)
    grad_gain = lax.optimization_barrier(jnp.sum(projection.astype(jnp.float32) * grad_proj, axis=1)) / student_gain
    return (loss, grad_gain, grad_proj)
```

```python
import jax
import jax.numpy as jnp
from jax import lax
from jax.sharding import Mesh, PartitionSpec as P

TW = 8192
EPS = 1e-06
F32, BF16 = jnp.float32, jnp.bfloat16
DP = ("xl", "z", "c")
TENSOR = ("y", "xh")


SWAP = [(0, 0), (1, 2), (2, 1), (3, 3)]
CROSS = [(c * 2 + xh, (1 - xh) * 2 + c) for c in (0, 1) for xh in (0, 1)]


def flip(x, axis, size, bit):
    return lax.ppermute(x, axis, [(i, i ^ bit) for i in range(size)])


def shift(x, axis, size, by):
    return lax.ppermute(x, axis, [(i, (i + by) % size) for i in range(size)])


def corner(flip_xl, flip_c, flip_xh):
    return [
        (xl * 4 + c * 2 + xh, (xl ^ flip_xl) * 4 + (xh ^ flip_c) * 2 + (c ^ flip_xh))
        for xl in (0, 1)
        for c in (0, 1)
        for xh in (0, 1)
    ]


def gather_projection(projection, lengths):
    xl, xh, z = lax.axis_index("xl"), lax.axis_index("xh"), lax.axis_index("z")
    length = lengths[0]
    lane = lax.broadcasted_iota(jnp.int32, (16, 512), 1)
    digits = jnp.where(lane == 0, length // 16, jnp.where(lane == 1, length % 16, 0)).astype(BF16)
    own = jnp.concatenate([projection, digits], axis=0)
    got = {}
    for fx in (0, 1):
        for fc in (0, 1):
            got[fx, fc] = lax.ppermute(own, ("xl", "c", "xh"), corner(fx, 0, fc))
    by_xl = []
    for x in (0, 1):
        for k in (0, 1):
            a = jnp.where(xh == k, got[0, 0], got[0, 1])
            b = jnp.where(xh == k, got[1, 0], got[1, 1])
            by_xl.append(jnp.where(xl == x, a, b))
    block = jnp.concatenate([b[:64] for b in by_xl] + [b[64:68] for b in by_xl], axis=0)
    shards = {0: block}
    up = down = block
    for step in (1, 2, 3):
        up = shift(up, "z", 8, 1)
        down = shift(down, "z", 8, -1)
        shards[-step], shards[step] = up, down
    first = shift(up[:128], "z", 8, 1)
    last = shift(down[128:], "z", 8, -1)
    shards[4] = jnp.concatenate([first, last], axis=0)
    full = jnp.zeros((2, 8, 128, 512), BF16)
    total = jnp.zeros((), F32)
    for offset, shard in shards.items():
        rows = shard[:256].reshape(2, 1, 128, 512)
        full = lax.dynamic_update_slice(full, rows, (0, (z + offset) % 8, 0, 0))
        tail = shard[256:].astype(F32)
        total += jnp.sum(tail.reshape(4, 4, 512)[:, 0, 0] * 16 + tail.reshape(4, 4, 512)[:, 0, 1])
    return full.reshape(2048, 512), total


def row_scale(teacher_hidden, teacher_gain, lengths):
    hidden_f = teacher_hidden.astype(F32)
    squares = jnp.sum(hidden_f * hidden_f, axis=1).reshape(16, 128)
    for bit in (1, 2, 4):
        squares = squares + flip(squares, "y", 8, bit)
    packed = jnp.concatenate(
        [
            squares,
            teacher_gain.astype(F32).reshape(4, 128),
            jnp.broadcast_to(lengths.astype(F32), (4, 128)),
        ],
        axis=0,
    )
    mine = lax.ppermute(packed, ("c", "xh"), SWAP)
    other = lax.ppermute(squares, ("c", "xh"), CROSS)
    scale = lax.rsqrt((mine[:16] + other).reshape(2048) / TW + EPS)
    return scale, mine[16:20].reshape(512), mine[20, 0].astype(jnp.int32)


def on_device(teacher_hidden, teacher_gain, student_hidden, student_gain, projection, lengths):
    c, xl, xh = lax.axis_index("c"), lax.axis_index("xl"), lax.axis_index("xh")
    student_f = student_hidden.astype(F32)
    normed = student_f * lax.rsqrt(jnp.mean(student_f * student_f, axis=1, keepdims=True) + EPS)
    scaled = (normed * student_gain).astype(BF16)
    scaled = lax.ppermute(scaled, ("c", "xh"), SWAP)
    near = lax.all_gather(scaled, "y", axis=0, tiled=True)

    proj_full, count = gather_projection(projection, lengths)
    scale, gain, length = row_scale(teacher_hidden, teacher_gain, lengths)
    teacher = lax.ppermute(teacher_hidden, ("c", "xh"), SWAP).reshape(8, 2, 128, 512)
    far = flip(near, "c", 2, 1)

    factor = 2.0 / count
    scale = scale.reshape(8, 2, 128)
    grad_total = None
    loss_part = jnp.zeros((), F32)
    for rows, half in ((near, c), (far, 1 - c)):
        hidden = lax.dynamic_index_in_dim(teacher, half, 1, keepdims=False).reshape(1024, 512)
        rs = lax.dynamic_index_in_dim(scale, half, 1, keepdims=False).reshape(1024, 1)
        target = hidden.astype(F32) * rs * gain
        predicted = jnp.dot(rows, proj_full, preferred_element_type=F32)
        i = jnp.arange(1024, dtype=jnp.int32)
        positions = (i // 128) * 256 + half * 128 + i % 128
        diff = jnp.where((positions < length)[:, None], predicted - target, F32(0.0))
        slope = (diff * factor).astype(BF16)
        part = jnp.dot(rows.T, slope, preferred_element_type=F32)
        grad_total = part if grad_total is None else grad_total + part
        loss_part += jnp.sum(diff * diff)

    gain_part = jnp.sum(proj_full.astype(F32) * grad_total, axis=1)
    by_z = grad_total.reshape(2, 8, 128, 512).transpose(1, 2, 0, 3).reshape(1024, 1024)
    mine = lax.psum_scatter(by_z, "z", scatter_dimension=0, tiled=True).reshape(2, 64, 2, 512)

    sums = jnp.concatenate(
        [gain_part.reshape(16, 128), jnp.broadcast_to(loss_part, (8, 128))], axis=0
    )
    for axis, size, bit in (
        ("c", 2, 1),
        ("z", 8, 1),
        ("z", 8, 2),
        ("z", 8, 4),
        ("y", 8, 1),
        ("y", 8, 2),
        ("y", 8, 4),
        ("xl", 2, 1),
        ("xh", 2, 1),
    ):
        sums = sums + flip(sums, axis, size, bit)
    grad_proj = jnp.zeros((64, 512), F32)
    for fx in (0, 1):
        for fc in (0, 1):
            send = lax.dynamic_slice(mine, (xh ^ fc, 0, xl ^ fx, 0), (1, 64, 1, 512)).reshape(64, 512)
            grad_proj += lax.ppermute(send, ("xl", "c", "xh"), corner(fx, fc, 0))
    loss = sums[16, 0] / (count * TW)
    grad_gain = sums[:16].reshape(2048) / student_gain
    return (loss, grad_gain, grad_proj)


def solution(mesh):
    parts = Mesh(mesh.devices.reshape(2, 8, 2, 8, 2), DP + TENSOR)
    return jax.shard_map(
        on_device,
        mesh=parts,
        in_specs=(P(DP, TENSOR), P(TENSOR), P(DP + TENSOR, None), P(), P(DP, TENSOR), P(DP)),
        out_specs=(P(), P(), P(DP, TENSOR)),
        check_vma=False,
    )
```

```python
import functools

import jax
import jax.numpy as jnp
from jax import lax
from jax.experimental import pallas as pl
from jax.experimental.pallas import tpu as pltpu
from jax.sharding import Mesh, PartitionSpec as P

TW = 8192
EPS = 1e-06
F32, BF16 = jnp.float32, jnp.bfloat16
DP = ("xl", "z", "c")
TENSOR = ("y", "xh")


SWAP = [(0, 0), (1, 2), (2, 1), (3, 3)]
CROSS = [(c * 2 + xh, (1 - xh) * 2 + c) for c in (0, 1) for xh in (0, 1)]


def flip(x, axis, size, bit):
    return lax.ppermute(x, axis, [(i, i ^ bit) for i in range(size)])


def shift(x, axis, size, by):
    return lax.ppermute(x, axis, [(i, (i + by) % size) for i in range(size)])


def corner(flip_xl, flip_c):
    return [
        (xl * 4 + c * 2 + xh, (xl ^ flip_xl) * 4 + (xh ^ flip_c) * 2 + c)
        for xl in (0, 1)
        for c in (0, 1)
        for xh in (0, 1)
    ]


def tie(*arrays):
    return lax.optimization_barrier(arrays)


def rows_step(ints, half, factor, rows, proj_ref, teacher_lo, teacher_hi, scale_ref, gain_ref, grad_ref, loss_ref, blocks):
    step = pl.program_id(0)
    length = ints[1]
    predicted = jnp.dot(rows, proj_ref[...], preferred_element_type=F32)
    scale = jnp.concatenate([scale_ref[...], jnp.zeros((112, 128), F32)], axis=0).T
    lane = lax.broadcasted_iota(jnp.int32, (128, 128), 1)
    row = lax.broadcasted_iota(jnp.int32, (128, 1), 0)
    gain = gain_ref[...]
    loss = jnp.zeros((8, 512), F32)
    slopes = []
    for b in range(blocks):
        place = (step * blocks + b) * 2 + half
        s = jnp.sum(jnp.where(lane == place, scale, 0.0), axis=1, keepdims=True)
        hidden = jnp.where(step == 0, teacher_lo[b, 0], teacher_hi[b, 0])
        target = hidden.astype(F32) * s * gain
        valid = (place * 128 + row) < length
        diff = jnp.where(valid, predicted[b * 128 : (b + 1) * 128] - target, 0.0)
        slopes.append((diff * factor).astype(BF16))
        loss += jnp.sum((diff * diff).reshape(16, 8, 512), axis=0)
    slope = jnp.concatenate(slopes, axis=0)
    loss_ref[...] += loss[:, :128] + loss[:, 128:256] + loss[:, 256:384] + loss[:, 384:]
    for x in range(2):
        grad_ref[:, x * 512 : (x + 1) * 512] += lax.dot_general(
            rows[:, x * 1024 : (x + 1) * 1024],
            slope,
            (((0,), (0,)), ((), ())),
            preferred_element_type=F32,
        )


def near_kernel(ints, rows_ref, teacher_lo, teacher_hi, scale_ref, gain_ref, *rest, blocks):
    shards, (grad_ref, loss_ref, proj_ref, count_ref) = rest[:9], rest[9:]

    @pl.when(pl.program_id(0) == 0)
    def _():
        z = ints[2]
        tails = jnp.zeros((16, 512), F32)
        for offset, shard in zip((0, 1, 2, 3, -1, -2, -3), shards):
            place = lax.rem(z + (offset + 8), 8) * 128
            for x in range(2):
                proj_ref[pl.ds(pl.multiple_of(x * 1024 + place, 128), 128), :] = shard[x * 128 : (x + 1) * 128, :]
            tails += shard[256:272, :].astype(F32)
        place = lax.rem(z + 4, 8) * 128
        proj_ref[pl.ds(pl.multiple_of(place, 128), 128), :] = shards[7][...]
        proj_ref[pl.ds(pl.multiple_of(1024 + place, 128), 128), :] = shards[8][:128, :]
        tails += shards[8][128:144, :].astype(F32)
        lane = lax.broadcasted_iota(jnp.int32, (16, 512), 1)
        weight = jnp.where(lane == 0, 4.0, jnp.where(lane == 1, 0.25, 0.0))
        count_ref[...] = jnp.full((8, 128), jnp.sum(tails * weight), F32)
        grad_ref[...] = jnp.zeros_like(grad_ref)
        loss_ref[...] = jnp.zeros_like(loss_ref)

    factor = 2.0 / count_ref[0:1, 0:1]
    rows_step(
        ints, ints[0], factor, rows_ref[...], proj_ref, teacher_lo, teacher_hi, scale_ref, gain_ref, grad_ref, loss_ref, blocks
    )


def far_kernel(ints, rows_ref, teacher_lo, teacher_hi, scale_ref, gain_ref, *rest, blocks):
    proj_ref, count_ref, grad_in, loss_in, grad_ref, loss_ref, sums_ref = rest

    @pl.when(pl.program_id(0) == 0)
    def _():
        grad_ref[...] = grad_in[...]
        loss_ref[...] = loss_in[...]

    factor = 2.0 / count_ref[0:1, 0:1]
    rows_step(
        ints, 1 - ints[0], factor, rows_ref[...], proj_ref, teacher_lo, teacher_hi, scale_ref, gain_ref, grad_ref, loss_ref, blocks
    )

    @pl.when(pl.program_id(0) == pl.num_programs(0) - 1)
    def _():
        for x in range(2):
            g = grad_ref[:, x * 512 : (x + 1) * 512] * proj_ref[x * 1024 : (x + 1) * 1024, :].astype(F32)
            g = g[:, :128] + g[:, 128:256] + g[:, 256:384] + g[:, 384:]
            sums_ref[x * 8 : (x + 1) * 8, :] = jnp.sum(g.reshape(8, 128, 128), axis=2)
        sums_ref[16:24, :] = loss_ref[...]


def whole(shape):
    return pl.BlockSpec(shape, lambda i, ints: (0,) * len(shape), pipeline_mode=pl.Buffered(1))


def rows_call(kernel, name, flipped, ints, rows, teacher, scale, gain, extra, outs, blocks=4):
    half = (lambda i, ints: (0, 1 - ints[0], 0, 0)) if flipped else (lambda i, ints: (0, ints[0], 0, 0))
    return pl.pallas_call(
        functools.partial(kernel, blocks=blocks),
        grid_spec=pltpu.PrefetchScalarGridSpec(
            num_scalar_prefetch=1,
            grid=(8 // blocks,),
            in_specs=[
                pl.BlockSpec((blocks * 128, 2048), lambda i, ints: (i, 0)),
                pl.BlockSpec((4, 1, 128, 512), half, pipeline_mode=pl.Buffered(1)),
                pl.BlockSpec((4, 1, 128, 512), half, pipeline_mode=pl.Buffered(1)),
                whole((16, 128)),
                whole((1, 512)),
            ]
            + [whole(a.shape) for a in extra],
            out_specs=[whole(shape) for shape, _ in outs],
        ),
        out_shape=[jax.ShapeDtypeStruct(shape, dtype) for shape, dtype in outs],
        compiler_params=pltpu.CompilerParams(vmem_limit_bytes=28 * 2**20),
        cost_estimate=pl.CostEstimate(flops=4 * 1024 * 2048 * 512, bytes_accessed=12 * 2**20, transcendentals=0),
        name=name,
    )(ints, rows, *teacher, scale, gain, *extra)


def own_rows(projection, lengths):
    length = lengths[0]
    lane = lax.broadcasted_iota(jnp.int32, (16, 512), 1)
    digits = jnp.where(lane == 0, length >> 4, jnp.where(lane == 1, length & 15, 0)).astype(BF16)
    return jnp.concatenate([projection, digits], axis=0)


def projection_block(rows_of_x, c):
    rows_of_x = rows_of_x.reshape(2, 2, 80, 512)
    kept = lax.dynamic_index_in_dim(rows_of_x, c, 1, keepdims=False)
    given = lax.dynamic_index_in_dim(rows_of_x, 1 - c, 1, keepdims=False)
    taken = flip(given, "c", 2, 1)
    low, high = jnp.where(c == 0, kept, taken), jnp.where(c == 0, taken, kept)
    parts = [low[0], high[0], low[1], high[1]]
    return jnp.concatenate([p[:64] for p in parts] + [p[64:68] for p in parts], axis=0)


def on_device(teacher_hidden, teacher_gain, student_hidden, student_gain, projection, lengths):
    c, xl, xh, z = (lax.axis_index(a) for a in ("c", "xl", "xh", "z"))
    student_f = student_hidden.astype(F32)
    normed = student_f * lax.rsqrt(jnp.mean(student_f * student_f, axis=1, keepdims=True) + EPS)
    scaled = (normed * student_gain).astype(BF16)
    scaled = lax.ppermute(scaled, ("c", "xh"), SWAP)
    rows_of_x = lax.all_gather(own_rows(projection, lengths), ("xl", "xh"), axis=0, tiled=True)
    scaled, rows_of_x = tie(scaled, rows_of_x)
    near = lax.all_gather(scaled, "y", axis=0, tiled=True)

    block = projection_block(rows_of_x, c)
    up1, down1 = shift(block, "z", 8, 1), shift(block, "z", 8, -1)

    hidden_f = teacher_hidden.astype(F32)
    squares = jnp.sum(hidden_f * hidden_f, axis=1).reshape(16, 128)
    squares, _ = tie(squares, block)
    squares = lax.psum(squares, "y")
    packed = jnp.concatenate(
        [
            squares,
            teacher_gain.astype(F32).reshape(4, 128),
            jnp.broadcast_to(lengths.astype(F32), (4, 128)),
        ],
        axis=0,
    )
    mine = lax.ppermute(packed, ("c", "xh"), SWAP)
    other = lax.ppermute(squares, ("c", "xh"), CROSS)
    teacher, _ = tie(teacher_hidden, block)
    lo = lax.ppermute(teacher[:1024], ("c", "xh"), SWAP)

    up1, down1, squares, lo = tie(up1, down1, squares, lo)
    hi = lax.ppermute(teacher[1024:], ("c", "xh"), SWAP)
    up2, down2 = shift(up1, "z", 8, 1), shift(down1, "z", 8, -1)
    up2, down2, mine, other = tie(up2, down2, mine, other)
    up3, down3 = shift(up2, "z", 8, 1), shift(down2, "z", 8, -1)
    up3, down3, hi = tie(up3, down3, hi)
    teacher = [lo.reshape(4, 2, 128, 512), hi.reshape(4, 2, 128, 512)]
    up4 = shift(up3[:128], "z", 8, 1)
    down4 = shift(down3[128:], "z", 8, -1)
    near, up4, down4 = tie(near, up4, down4)
    far = flip(near, "c", 2, 1)

    scale = lax.rsqrt((mine[:16] + other) / TW + EPS)
    gain = mine[16:20].reshape(1, 512)
    ints = jnp.stack([c, mine[20, 0].astype(jnp.int32), z]).astype(jnp.int32)
    grad, loss_part, proj_full, count = rows_call(
        near_kernel,
        "near_rows",
        False,
        ints,
        near,
        teacher,
        scale,
        gain,
        [block, down1, down2, down3, up1, up2, up3, up4, down4],
        [((1024, 1024), F32), ((8, 128), F32), ((2048, 512), BF16), ((8, 128), F32)],
    )
    grad, _, sums = rows_call(
        far_kernel,
        "far_rows",
        True,
        ints,
        far,
        teacher,
        scale,
        gain,
        [proj_full, count, grad, loss_part],
        [((1024, 1024), F32), ((8, 128), F32), ((24, 128), F32)],
    )
    mine = lax.psum_scatter(grad, "z", scatter_dimension=0, tiled=True).reshape(2, 64, 2, 512)

    for axis, size, bit in (
        ("c", 2, 1),
        ("z", 8, 1),
        ("z", 8, 2),
        ("z", 8, 4),
        ("y", 8, 1),
        ("y", 8, 2),
        ("y", 8, 4),
        ("xl", 2, 1),
        ("xh", 2, 1),
    ):
        sums = sums + flip(sums, axis, size, bit)
    grad_proj = jnp.zeros((64, 512), F32)
    for fx in (0, 1):
        for fc in (0, 1):
            send = lax.dynamic_slice(mine, (xh ^ fc, 0, xl ^ fx, 0), (1, 64, 1, 512)).reshape(64, 512)
            grad_proj += lax.ppermute(send, ("xl", "c", "xh"), corner(fx, fc))
    loss = jnp.sum(sums[16:]) / (count[0, 0] * TW)
    grad_gain = sums[:16].reshape(2048) / student_gain
    return (loss, grad_gain, grad_proj)


def solution(mesh):
    parts = Mesh(mesh.devices.reshape(2, 8, 2, 8, 2), DP + TENSOR)
    return jax.shard_map(
        on_device,
        mesh=parts,
        in_specs=(P(DP, TENSOR), P(TENSOR), P(DP + TENSOR, None), P(), P(DP, TENSOR), P(DP)),
        out_specs=(P(), P(), P(DP, TENSOR)),
        check_vma=False,
    )
```

```python
import jax
import jax.numpy as jnp
from jax import lax
from jax.experimental import pallas as pl
from jax.experimental.pallas import tpu as pltpu
from jax.sharding import Mesh, PartitionSpec as P

TW = 8192
EPS = 1e-06
WIDE = 2176
F32, BF16 = jnp.float32, jnp.bfloat16
DP = ("xl", "z", "c")
TENSOR = ("y", "xh")


SWAP = [(0, 0), (1, 2), (2, 1), (3, 3)]


CROSS = [(c * 2 + xh, (1 - xh) * 2 + c) for c in (0, 1) for xh in (0, 1)]
VMEM = pl.BlockSpec(memory_space=pltpu.VMEM)
SMEM = pl.BlockSpec(memory_space=pltpu.SMEM)
HBM = pl.BlockSpec(memory_space=pltpu.HBM)


def flip(x, axis, size, bit):
    return lax.ppermute(x, axis, [(i, i ^ bit) for i in range(size)])


def shift(x, axis, size, by):
    return lax.ppermute(x, axis, [(i, (i + by) % size) for i in range(size)])


def corner(flip_xl, flip_c):
    return [
        (xl * 4 + c * 2 + xh, (xl ^ flip_xl) * 4 + (xh ^ flip_c) * 2 + c)
        for xl in (0, 1)
        for c in (0, 1)
        for xh in (0, 1)
    ]


def tie(*arrays):
    return lax.optimization_barrier(arrays)


def call(kernel, name, in_specs, out_specs, outs, scratch, flops, *args):
    return pl.pallas_call(
        kernel,
        in_specs=in_specs,
        out_specs=out_specs,
        out_shape=[jax.ShapeDtypeStruct(shape, dtype) for shape, dtype in outs],
        scratch_shapes=scratch,
        compiler_params=pltpu.CompilerParams(vmem_limit_bytes=20 * 2**20),
        cost_estimate=pl.CostEstimate(flops=flops, bytes_accessed=6 * 2**20, transcendentals=0),
        name=name,
    )(*args)


def put_parts(out_ref, x):
    for part in range(3):
        rounded = x.astype(BF16)
        out_ref[part * 16 : part * 16 + 16, 2048:] = rounded
        x = x - rounded.astype(F32)


def head_kernel(teacher_ref, student_ref, student_gain_ref, out_ref, squares_ref):
    student_f = student_ref[...].astype(F32)
    mean = jnp.sum(student_f * student_f, axis=1, keepdims=True) / 2048
    out_ref[:, :2048] = (student_f * lax.rsqrt(mean + EPS) * student_gain_ref[...]).astype(BF16)
    out_ref[:, 2048:] = jnp.zeros((128, 128), BF16)
    squares = []
    for i in range(16):
        t = teacher_ref[i * 128 : (i + 1) * 128, :].astype(F32)
        t = t * t
        t = t[:, :128] + t[:, 128:256] + t[:, 256:384] + t[:, 384:]
        squares.append(jnp.sum(t.T, axis=0, keepdims=True))
    squares = jnp.concatenate(squares, axis=0)
    squares_ref[...] = squares
    put_parts(out_ref, squares)


def join_kernel(rows_ref, cross_ref, out_ref, buffer, sem):
    buffer[...] = rows_ref[...]
    squares = cross_ref[...]
    for part in (2, 1, 0):
        squares += rows_ref[part * 16 : part * 16 + 16, 2048:].astype(F32)
    put_parts(buffer, squares)
    copy = pltpu.make_async_copy(buffer, out_ref, sem)
    copy.start()
    copy.wait()


def place_kernel(z_ref, *rest):
    shards, (proj_ref, count_ref) = rest[:9], rest[9:]
    z = z_ref[0]
    tails = jnp.zeros((16, 512), F32)
    for offset, shard in zip((0, 1, 2, 3, -1, -2, -3), shards):
        at = lax.rem(z + (offset + 8), 8) * 128
        for x in range(2):
            proj_ref[pl.ds(pl.multiple_of(x * 1024 + at, 128), 128), :] = shard[x * 128 : (x + 1) * 128, :]
        tails += shard[256:272, :].astype(F32)
    at = lax.rem(z + 4, 8) * 128
    proj_ref[pl.ds(pl.multiple_of(at, 128), 128), :] = shards[7][...]
    proj_ref[pl.ds(pl.multiple_of(1024 + at, 128), 128), :] = shards[8][:128, :]
    tails += shards[8][128:144, :].astype(F32)
    lane = lax.broadcasted_iota(jnp.int32, (16, 512), 1)
    weight = jnp.where(lane == 0, 4.0, jnp.where(lane == 1, 0.25, 0.0))
    count_ref[...] = jnp.full((8, 128), jnp.sum(tails * weight), F32)


def load_rows(rows_hbm, rows, sems):
    copies = [
        pltpu.make_async_copy(rows_hbm.at[pl.ds(i * 4, 4)], rows.at[pl.ds(i * 4, 4)], sems.at[i]) for i in range(2)
    ]
    for copy in copies:
        copy.start()
    return copies


def slopes(i, half, length, factor, rows, proj_ref, teacher_ref, scale, gain):
    predicted = jnp.dot(rows, proj_ref[...], preferred_element_type=F32)
    lane = lax.broadcasted_iota(jnp.int32, (128, 128), 1)
    row = lax.broadcasted_iota(jnp.int32, (128, 1), 0)
    loss = jnp.zeros((8, 512), F32)
    found = []
    for b in range(4):
        place = (i * 4 + b) * 2 + half
        s = jnp.sum(jnp.where(lane == place, scale, 0.0), axis=1, keepdims=True)
        target = teacher_ref[i * 4 + b, half].astype(F32) * s * gain
        valid = (place * 128 + row) < length
        diff = jnp.where(valid, predicted[b * 128 : (b + 1) * 128] - target, 0.0)
        found.append((diff * factor).astype(BF16))
        loss += jnp.sum((diff * diff).reshape(16, 8, 512), axis=0)
    loss = loss[:, :128] + loss[:, 128:256] + loss[:, 256:384] + loss[:, 384:]
    return jnp.concatenate(found, axis=0), loss


def grad_part(rows, slope, x):
    return lax.dot_general(
        rows[:, x * 1024 : (x + 1) * 1024], slope, (((0,), (0,)), ((), ())), preferred_element_type=F32
    )


def columns(scale):
    return jnp.concatenate([scale, jnp.zeros((112, 128), F32)], axis=0).T


def near_kernel(ints, rows_hbm, proj_ref, count_ref, teacher_ref, gain_ref, *rest):
    grad_ref, loss_ref, scale_ref, rows_ref, notes, sems = rest
    notes_copy = pltpu.make_async_copy(rows_hbm.at[:, pl.ds(0, 48), pl.ds(2048, 128)], notes, sems.at[2])
    notes_copy.start()
    copies = load_rows(rows_hbm, rows_ref, sems)
    notes_copy.wait()
    squares = jnp.zeros((16, 128), F32)
    for part in (2, 1, 0):
        for y in range(8):
            squares += notes[y, part * 16 : part * 16 + 16, :].astype(F32)
    scale = lax.rsqrt(squares / TW + EPS)
    scale_ref[...] = scale
    scale = columns(scale)
    factor = 2.0 / count_ref[0:1, 0:1]
    for i in range(2):
        copies[i].wait()
        rows = rows_ref[i * 4 : i * 4 + 4, :, :2048].reshape(512, 2048)
        slope, loss = slopes(i, ints[0], ints[1], factor, rows, proj_ref, teacher_ref, scale, gain_ref[...])
        loss_ref[...] = loss if i == 0 else loss_ref[...] + loss
        for x in range(2):
            lanes = slice(x * 512, (x + 1) * 512)
            part = grad_part(rows, slope, x)
            grad_ref[:, lanes] = part if i == 0 else grad_ref[:, lanes] + part


def far_kernel(ints, rows_hbm, proj_ref, count_ref, teacher_ref, gain_ref, *rest):
    scale_ref, grad_in, loss_in, grad_hbm, sums_ref, rows_ref, total, sems = rest
    copies = load_rows(rows_hbm, rows_ref, sems)
    scale = columns(scale_ref[...])
    factor = 2.0 / count_ref[0:1, 0:1]
    sums_ref[16:24, :] = loss_in[...]
    out = []
    for i in range(2):
        copies[i].wait()
        rows = rows_ref[i * 4 : i * 4 + 4, :, :2048].reshape(512, 2048)
        slope, loss = slopes(i, 1 - ints[0], ints[1], factor, rows, proj_ref, teacher_ref, scale, gain_ref[...])
        sums_ref[16:24, :] += loss
        for x in range(2):
            lanes = slice(x * 512, (x + 1) * 512)
            part = grad_part(rows, slope, x)
            total[x] = (grad_in[:, lanes] if i == 0 else total[x]) + part
            if i == 1:
                copy = pltpu.make_async_copy(total.at[x], grad_hbm.at[:, pl.ds(x * 512, 512)], sems.at[2 + x])
                copy.start()
                out.append(copy)
    for x in range(2):
        g = total[x] * proj_ref[x * 1024 : (x + 1) * 1024, :].astype(F32)
        g = g[:, :128] + g[:, 128:256] + g[:, 256:384] + g[:, 384:]
        sums_ref[x * 8 : (x + 1) * 8, :] = jnp.sum(g.reshape(8, 128, 128), axis=2)
    for copy in out:
        copy.wait()


def own_rows(projection, teacher_gain, lengths):
    length = lengths[0]
    lane = lax.broadcasted_iota(jnp.int32, (8, 512), 1)
    digits = jnp.where(lane == 0, length >> 4, jnp.where(lane == 1, length & 15, 0)).astype(BF16)
    return jnp.concatenate([projection, digits, jnp.broadcast_to(teacher_gain, (8, 512))], axis=0)


def projection_flips(own):
    return [
        lax.ppermute(own, ("xl", "xh"), [(i, i ^ (fx * 2 + fc)) for i in range(4)]) for fx, fc in ((0, 1), (1, 0), (1, 1))
    ]


def projection_block(own, by_xh, by_xl, by_both):
    xl, xh = lax.axis_index("xl"), lax.axis_index("xh")
    parts = []
    for x in (0, 1):
        for k in (0, 1):
            a = jnp.where(xh == k, own, by_xh)
            b = jnp.where(xh == k, by_xl, by_both)
            parts.append(jnp.where(xl == x, a, b))
    return jnp.concatenate([p[:64] for p in parts] + [p[64:68] for p in parts], axis=0)


def on_device(teacher_hidden, teacher_gain, student_hidden, student_gain, projection, lengths):
    c, xl, xh, z = (lax.axis_index(a) for a in ("c", "xl", "xh", "z"))
    own = lax.ppermute(own_rows(projection, teacher_gain, lengths), ("c", "xh"), SWAP)
    scaled, squares = call(
        head_kernel,
        "head",
        [VMEM] * 3,
        [VMEM] * 2,
        [((128, WIDE), BF16), ((16, 128), F32)],
        [],
        10**7,
        teacher_hidden,
        student_hidden,
        student_gain.reshape(1, 2048),
    )
    scaled, squares, own = tie(scaled, squares, own)
    scaled = lax.ppermute(scaled, ("c", "xh"), SWAP)
    cross = lax.ppermute(squares, ("c", "xh"), CROSS)
    flips = projection_flips(own)
    scaled, cross, *flips = tie(scaled, cross, *flips)
    (joined,) = call(
        join_kernel,
        "join",
        [VMEM] * 2,
        [HBM],
        [((128, WIDE), BF16)],
        [pltpu.VMEM((128, WIDE), BF16), pltpu.SemaphoreType.DMA],
        10**5,
        scaled,
        cross,
    )
    near = lax.all_gather(joined, "y", axis=0, tiled=True)

    flips, _ = tie(flips, joined)
    block = projection_block(own, *flips)
    up1, down1 = shift(block, "z", 8, 1), shift(block, "z", 8, -1)
    teacher, _ = tie(teacher_hidden, block)
    teacher = lax.ppermute(teacher, ("c", "xh"), SWAP)
    up2, down2 = shift(up1, "z", 8, 1), shift(down1, "z", 8, -1)
    up3, down3 = shift(up2, "z", 8, 1), shift(down2, "z", 8, -1)
    up3, down3, teacher = tie(up3, down3, teacher)
    teacher = teacher.reshape(8, 2, 128, 512)
    up4 = shift(up3[:128], "z", 8, 1)
    down4 = shift(down3[128:], "z", 8, -1)
    proj_full, count = call(
        place_kernel,
        "place",
        [SMEM] + [VMEM] * 9,
        [VMEM] * 2,
        [((2048, 512), BF16), ((8, 128), F32)],
        [],
        10**6,
        z.reshape(1),
        *(block, down1, down2, down3, up1, up2, up3, up4, down4),
    )
    gain = own[72:73].astype(F32)
    length = (own[64, 0].astype(F32) * 16 + own[64, 1].astype(F32)).astype(jnp.int32)
    ints = jnp.stack([c, length]).astype(jnp.int32)
    near, proj_full, ints, gain = tie(near, proj_full, ints, gain)
    far = flip(near, "c", 2, 1)
    grad, loss_part, scale = call(
        near_kernel,
        "near_rows",
        [SMEM, HBM] + [VMEM] * 4,
        [VMEM] * 3,
        [((1024, 1024), F32), ((8, 128), F32), ((16, 128), F32)],
        [pltpu.VMEM((8, 128, WIDE), BF16), pltpu.VMEM((8, 48, 128), BF16), pltpu.SemaphoreType.DMA((3,))],
        4 * 1024 * 2048 * 512,
        *(ints, near.reshape(8, 128, WIDE), proj_full, count, teacher, gain),
    )
    grad, sums = call(
        far_kernel,
        "far_rows",
        [SMEM, HBM] + [VMEM] * 7,
        [HBM, VMEM],
        [((1024, 1024), F32), ((24, 128), F32)],
        [pltpu.VMEM((8, 128, WIDE), BF16), pltpu.VMEM((2, 1024, 512), F32), pltpu.SemaphoreType.DMA((4,))],
        4 * 1024 * 2048 * 512,
        *(ints, far.reshape(8, 128, WIDE), proj_full, count, teacher, gain, scale, grad, loss_part),
    )
    mine = lax.psum_scatter(grad, "z", scatter_dimension=0, tiled=True)

    for axis, size, bit in (
        ("c", 2, 1),
        ("z", 8, 1),
        ("z", 8, 2),
        ("z", 8, 4),
        ("y", 8, 1),
        ("y", 8, 2),
        ("y", 8, 4),
        ("xl", 2, 1),
        ("xh", 2, 1),
    ):
        sums = sums + flip(sums, axis, size, bit)
    grad_proj = jnp.zeros((64, 512), F32)
    for fx in (0, 1):
        for fc in (0, 1):
            send = lax.dynamic_slice(mine, ((xh ^ fc) * 64, (xl ^ fx) * 512), (64, 512))
            grad_proj += lax.ppermute(send, ("xl", "c", "xh"), corner(fx, fc))
    loss = jnp.sum(sums[16:]) / (count[0, 0] * TW)
    grad_gain = sums[:16].reshape(2048) / student_gain
    return (loss, grad_gain, grad_proj)


def solution(mesh):
    parts = Mesh(mesh.devices.reshape(2, 8, 2, 8, 2), DP + TENSOR)
    return jax.shard_map(
        on_device,
        mesh=parts,
        in_specs=(P(DP, TENSOR), P(TENSOR), P(DP + TENSOR, None), P(), P(DP, TENSOR), P(DP)),
        out_specs=(P(), P(), P(DP, TENSOR)),
        check_vma=False,
    )
```

```python
import jax
import jax.numpy as jnp
from jax import lax
from jax.experimental import pallas as pl
from jax.experimental.pallas import tpu as pltpu
from jax.sharding import Mesh, PartitionSpec as P

TW = 8192
EPS = 1e-06
WIDE = 2176
F32, BF16 = jnp.float32, jnp.bfloat16
DP = ("xl", "z", "c")
TENSOR = ("y", "xh")


SWAP = [(0, 0), (1, 2), (2, 1), (3, 3)]


CROSS = [(c * 2 + xh, (1 - xh) * 2 + c) for c in (0, 1) for xh in (0, 1)]
VMEM = pl.BlockSpec(memory_space=pltpu.VMEM)
SMEM = pl.BlockSpec(memory_space=pltpu.SMEM)
HBM = pl.BlockSpec(memory_space=pltpu.HBM)


def flip(x, axis, size, bit):
    return lax.ppermute(x, axis, [(i, i ^ bit) for i in range(size)])


def shift(x, axis, size, by):
    return lax.ppermute(x, axis, [(i, (i + by) % size) for i in range(size)])


def corner(flip_xl, flip_c):
    return [
        (xl * 4 + c * 2 + xh, (xl ^ flip_xl) * 4 + (xh ^ flip_c) * 2 + c)
        for xl in (0, 1)
        for c in (0, 1)
        for xh in (0, 1)
    ]


def tie(*arrays):
    return lax.optimization_barrier(arrays)


def call(kernel, name, in_specs, out_specs, outs, scratch, flops, *args):
    return pl.pallas_call(
        kernel,
        in_specs=in_specs,
        out_specs=out_specs,
        out_shape=[jax.ShapeDtypeStruct(shape, dtype) for shape, dtype in outs],
        scratch_shapes=scratch,
        compiler_params=pltpu.CompilerParams(vmem_limit_bytes=16 * 2**20),
        cost_estimate=pl.CostEstimate(flops=flops, bytes_accessed=6 * 2**20, transcendentals=0),
        name=name,
    )(*args)


def put_parts(out_ref, x):
    for part in range(3):
        rounded = x.astype(BF16)
        out_ref[part * 16 : part * 16 + 16, 2048:] = rounded
        x = x - rounded.astype(F32)


def head_kernel(teacher_ref, student_ref, student_gain_ref, out_ref, squares_ref):
    student_f = student_ref[...].astype(F32)
    mean = jnp.sum(student_f * student_f, axis=1, keepdims=True) / 2048
    out_ref[:, :2048] = (student_f * lax.rsqrt(mean + EPS) * student_gain_ref[...]).astype(BF16)
    out_ref[:, 2048:] = jnp.zeros((128, 128), BF16)
    squares = []
    for i in range(16):
        t = teacher_ref[i * 128 : (i + 1) * 128, :].astype(F32)
        t = t * t
        t = t[:, :128] + t[:, 128:256] + t[:, 256:384] + t[:, 384:]
        squares.append(jnp.sum(t.T, axis=0, keepdims=True))
    squares = jnp.concatenate(squares, axis=0)
    squares_ref[...] = squares
    put_parts(out_ref, squares)


def join_kernel(rows_ref, cross_ref, out_ref, buffer, sem):
    buffer[...] = rows_ref[...]
    squares = cross_ref[...]
    for part in (2, 1, 0):
        squares += rows_ref[part * 16 : part * 16 + 16, 2048:].astype(F32)
    put_parts(buffer, squares)
    copy = pltpu.make_async_copy(buffer, out_ref, sem)
    copy.start()
    copy.wait()


def place_kernel(z_ref, *rest):
    shards, (proj_ref, count_ref) = rest[:9], rest[9:]
    z = z_ref[0]
    tails = jnp.zeros((16, 512), F32)
    for offset, shard in zip((0, 1, 2, 3, -1, -2, -3), shards):
        at = lax.rem(z + (offset + 8), 8) * 128
        for x in range(2):
            proj_ref[pl.ds(pl.multiple_of(x * 1024 + at, 128), 128), :] = shard[x * 128 : (x + 1) * 128, :]
        tails += shard[256:272, :].astype(F32)
    at = lax.rem(z + 4, 8) * 128
    proj_ref[pl.ds(pl.multiple_of(at, 128), 128), :] = shards[7][...]
    proj_ref[pl.ds(pl.multiple_of(1024 + at, 128), 128), :] = shards[8][:128, :]
    tails += shards[8][128:144, :].astype(F32)
    lane = lax.broadcasted_iota(jnp.int32, (16, 512), 1)
    weight = jnp.where(lane == 0, 4.0, jnp.where(lane == 1, 0.25, 0.0))
    count_ref[...] = jnp.full((8, 128), jnp.sum(tails * weight), F32)


def load_rows(rows_hbm, rows, sems):
    copies = [
        pltpu.make_async_copy(rows_hbm.at[pl.ds(i * 4, 4)], rows.at[pl.ds(i * 4, 4)], sems.at[i]) for i in range(2)
    ]
    for copy in copies:
        copy.start()
    return copies


def slopes(i, half, length, factor, rows, proj_ref, teacher_ref, scale, gain):
    predicted = jnp.dot(rows, proj_ref[...], preferred_element_type=F32)
    lane = lax.broadcasted_iota(jnp.int32, (128, 128), 1)
    row = lax.broadcasted_iota(jnp.int32, (128, 1), 0)
    loss = jnp.zeros((8, 512), F32)
    found = []
    for b in range(4):
        place = (i * 4 + b) * 2 + half
        s = jnp.sum(jnp.where(lane == place, scale, 0.0), axis=1, keepdims=True)
        target = teacher_ref[i * 4 + b, half].astype(F32) * s * gain
        valid = (place * 128 + row) < length
        diff = jnp.where(valid, predicted[b * 128 : (b + 1) * 128] - target, 0.0)
        found.append((diff * factor).astype(BF16))
        loss += jnp.sum((diff * diff).reshape(16, 8, 512), axis=0)
    loss = loss[:, :128] + loss[:, 128:256] + loss[:, 256:384] + loss[:, 384:]
    return jnp.concatenate(found, axis=0), loss


def grad_part(rows, slope, x):
    return lax.dot_general(
        rows[:, x * 1024 : (x + 1) * 1024], slope, (((0,), (0,)), ((), ())), preferred_element_type=F32
    )


def columns(scale):
    return jnp.concatenate([scale, jnp.zeros((112, 128), F32)], axis=0).T


def near_kernel(ints, rows_hbm, proj_ref, count_ref, teacher_ref, gain_ref, *rest):
    grad_ref, loss_ref, scale_ref, rows_ref, notes, sems = rest
    notes_copy = pltpu.make_async_copy(rows_hbm.at[:, pl.ds(0, 48), pl.ds(2048, 128)], notes, sems.at[2])
    notes_copy.start()
    copies = load_rows(rows_hbm, rows_ref, sems)
    notes_copy.wait()
    squares = jnp.zeros((16, 128), F32)
    for part in (2, 1, 0):
        for y in range(8):
            squares += notes[y, part * 16 : part * 16 + 16, :].astype(F32)
    scale = lax.rsqrt(squares / TW + EPS)
    scale_ref[...] = scale
    scale = columns(scale)
    factor = 2.0 / count_ref[0:1, 0:1]
    for i in range(2):
        copies[i].wait()
        rows = rows_ref[i * 4 : i * 4 + 4, :, :2048].reshape(512, 2048)
        slope, loss = slopes(i, ints[0], ints[1], factor, rows, proj_ref, teacher_ref, scale, gain_ref[...])
        loss_ref[...] = loss if i == 0 else loss_ref[...] + loss
        for x in range(2):
            lanes = slice(x * 512, (x + 1) * 512)
            part = grad_part(rows, slope, x)
            grad_ref[:, lanes] = part if i == 0 else grad_ref[:, lanes] + part


def far_kernel(ints, rows_hbm, proj_ref, count_ref, teacher_ref, gain_ref, *rest):
    scale_ref, grad_in, loss_in, grad_ref, sums_ref, rows_ref, sems = rest
    copies = load_rows(rows_hbm, rows_ref, sems)
    scale = columns(scale_ref[...])
    factor = 2.0 / count_ref[0:1, 0:1]
    sums_ref[16:24, :] = loss_in[...]
    for i in range(2):
        copies[i].wait()
        rows = rows_ref[i * 4 : i * 4 + 4, :, :2048].reshape(512, 2048)
        slope, loss = slopes(i, 1 - ints[0], ints[1], factor, rows, proj_ref, teacher_ref, scale, gain_ref[...])
        sums_ref[16:24, :] += loss
        for x in range(2):
            lanes = slice(x * 512, (x + 1) * 512)
            part = grad_part(rows, slope, x)
            grad_ref[:, lanes] = (grad_in[:, lanes] if i == 0 else grad_ref[:, lanes]) + part
    for x in range(2):
        g = grad_ref[:, x * 512 : (x + 1) * 512] * proj_ref[x * 1024 : (x + 1) * 1024, :].astype(F32)
        g = g[:, :128] + g[:, 128:256] + g[:, 256:384] + g[:, 384:]
        sums_ref[x * 8 : (x + 1) * 8, :] = jnp.sum(g.reshape(8, 128, 128), axis=2)


def own_rows(projection, teacher_gain, lengths):
    length = lengths[0]
    lane = lax.broadcasted_iota(jnp.int32, (8, 512), 1)
    digits = jnp.where(lane == 0, length >> 4, jnp.where(lane == 1, length & 15, 0)).astype(BF16)
    return jnp.concatenate([projection, digits, jnp.broadcast_to(teacher_gain, (8, 512))], axis=0)


def projection_flips(own):
    return [
        lax.ppermute(own, ("xl", "xh"), [(i, i ^ (fx * 2 + fc)) for i in range(4)]) for fx, fc in ((0, 1), (1, 0), (1, 1))
    ]


def projection_block(own, by_xh, by_xl, by_both):
    xl, xh = lax.axis_index("xl"), lax.axis_index("xh")
    parts = []
    for x in (0, 1):
        for k in (0, 1):
            a = jnp.where(xh == k, own, by_xh)
            b = jnp.where(xh == k, by_xl, by_both)
            parts.append(jnp.where(xl == x, a, b))
    return jnp.concatenate([p[:64] for p in parts] + [p[64:68] for p in parts], axis=0)


def on_device(teacher_hidden, teacher_gain, student_hidden, student_gain, projection, lengths):
    c, xl, xh, z = (lax.axis_index(a) for a in ("c", "xl", "xh", "z"))
    own = lax.ppermute(own_rows(projection, teacher_gain, lengths), ("c", "xh"), SWAP)
    scaled, squares = call(
        head_kernel,
        "head",
        [VMEM] * 3,
        [VMEM] * 2,
        [((128, WIDE), BF16), ((16, 128), F32)],
        [],
        10**7,
        teacher_hidden,
        student_hidden,
        student_gain.reshape(1, 2048),
    )
    scaled, squares, own = tie(scaled, squares, own)
    scaled = lax.ppermute(scaled, ("c", "xh"), SWAP)
    cross = lax.ppermute(squares, ("c", "xh"), CROSS)
    flips = projection_flips(own)
    scaled, cross, flips[0] = tie(scaled, cross, flips[0])
    (joined,) = call(
        join_kernel,
        "join",
        [VMEM] * 2,
        [HBM],
        [((128, WIDE), BF16)],
        [pltpu.VMEM((128, WIDE), BF16), pltpu.SemaphoreType.DMA],
        10**5,
        scaled,
        cross,
    )
    near = lax.all_gather(joined, "y", axis=0, tiled=True)

    block = projection_block(own, *flips)
    up1, down1 = shift(block, "z", 8, 1), shift(block, "z", 8, -1)
    teacher, _ = tie(teacher_hidden, block)
    teacher = lax.ppermute(teacher, ("c", "xh"), SWAP)
    up2, down2 = shift(up1, "z", 8, 1), shift(down1, "z", 8, -1)
    up3, down3 = shift(up2, "z", 8, 1), shift(down2, "z", 8, -1)
    up3, down3, teacher = tie(up3, down3, teacher)
    teacher = teacher.reshape(8, 2, 128, 512)
    up4 = shift(up3[:128], "z", 8, 1)
    down4 = shift(down3[128:], "z", 8, -1)
    proj_full, count = call(
        place_kernel,
        "place",
        [SMEM] + [VMEM] * 9,
        [VMEM] * 2,
        [((2048, 512), BF16), ((8, 128), F32)],
        [],
        10**6,
        z.reshape(1),
        *(block, down1, down2, down3, up1, up2, up3, up4, down4),
    )
    gain = own[72:73].astype(F32)
    length = (own[64, 0].astype(F32) * 16 + own[64, 1].astype(F32)).astype(jnp.int32)
    ints = jnp.stack([c, length]).astype(jnp.int32)
    near, proj_full, ints, gain = tie(near, proj_full, ints, gain)
    far = flip(near, "c", 2, 1)
    grad, loss_part, scale = call(
        near_kernel,
        "near_rows",
        [SMEM, HBM] + [VMEM] * 4,
        [VMEM] * 3,
        [((1024, 1024), F32), ((8, 128), F32), ((16, 128), F32)],
        [pltpu.VMEM((8, 128, WIDE), BF16), pltpu.VMEM((8, 48, 128), BF16), pltpu.SemaphoreType.DMA((3,))],
        4 * 1024 * 2048 * 512,
        *(ints, near.reshape(8, 128, WIDE), proj_full, count, teacher, gain),
    )
    grad, sums = call(
        far_kernel,
        "far_rows",
        [SMEM, HBM] + [VMEM] * 7,
        [VMEM] * 2,
        [((1024, 1024), F32), ((24, 128), F32)],
        [pltpu.VMEM((8, 128, WIDE), BF16), pltpu.SemaphoreType.DMA((2,))],
        4 * 1024 * 2048 * 512,
        *(ints, far.reshape(8, 128, WIDE), proj_full, count, teacher, gain, scale, grad, loss_part),
    )
    mine = lax.psum_scatter(grad, "z", scatter_dimension=0, tiled=True)

    for axis, size, bit in (
        ("c", 2, 1),
        ("z", 8, 1),
        ("z", 8, 2),
        ("z", 8, 4),
        ("y", 8, 1),
        ("y", 8, 2),
        ("y", 8, 4),
        ("xl", 2, 1),
        ("xh", 2, 1),
    ):
        sums = sums + flip(sums, axis, size, bit)
    mine, sums = tie(mine, sums)
    grad_proj = jnp.zeros((64, 512), F32)
    for fx in (0, 1):
        for fc in (0, 1):
            send = lax.dynamic_slice(mine, ((xh ^ fc) * 64, (xl ^ fx) * 512), (64, 512))
            grad_proj += lax.ppermute(send, ("xl", "c", "xh"), corner(fx, fc))
    loss = jnp.sum(sums[16:]) / (count[0, 0] * TW)
    grad_gain = sums[:16].reshape(2048) / student_gain
    return (loss, grad_gain, grad_proj)


def solution(mesh):
    parts = Mesh(mesh.devices.reshape(2, 8, 2, 8, 2), DP + TENSOR)
    return jax.shard_map(
        on_device,
        mesh=parts,
        in_specs=(P(DP, TENSOR), P(TENSOR), P(DP + TENSOR, None), P(), P(DP, TENSOR), P(DP)),
        out_specs=(P(), P(), P(DP, TENSOR)),
        check_vma=False,
    )
```

```python
import jax
import jax.numpy as jnp
from jax import lax
from jax.experimental import pallas as pl
from jax.experimental.pallas import tpu as pltpu
from jax.sharding import Mesh, PartitionSpec as P

TW = 8192
EPS = 1e-06
WIDE = 2176
F32, BF16 = jnp.float32, jnp.bfloat16
DP = ("xl", "z", "c")
TENSOR = ("y", "xh")


SWAP = [(0, 0), (1, 2), (2, 1), (3, 3)]


CROSS = [(c * 2 + xh, (1 - xh) * 2 + c) for c in (0, 1) for xh in (0, 1)]
VMEM = pl.BlockSpec(memory_space=pltpu.VMEM)
SMEM = pl.BlockSpec(memory_space=pltpu.SMEM)
HBM = pl.BlockSpec(memory_space=pltpu.HBM)


def flip(x, axis, size, bit):
    return lax.ppermute(x, axis, [(i, i ^ bit) for i in range(size)])


def shift(x, axis, size, by):
    return lax.ppermute(x, axis, [(i, (i + by) % size) for i in range(size)])


def across(flip_xl):
    return [
        (xl * 4 + c * 2 + xh, (xl ^ flip_xl) * 4 + xh * 2 + c) for xl in (0, 1) for c in (0, 1) for xh in (0, 1)
    ]


def tie(*arrays):
    return lax.optimization_barrier(arrays)


def call(kernel, name, in_specs, out_specs, outs, scratch, flops, *args):
    return pl.pallas_call(
        kernel,
        in_specs=in_specs,
        out_specs=out_specs,
        out_shape=[jax.ShapeDtypeStruct(shape, dtype) for shape, dtype in outs],
        scratch_shapes=scratch,
        compiler_params=pltpu.CompilerParams(vmem_limit_bytes=16 * 2**20),
        cost_estimate=pl.CostEstimate(flops=flops, bytes_accessed=6 * 2**20, transcendentals=0),
        name=name,
    )(*args)


def put_parts(out_ref, x):
    for part in range(3):
        rounded = x.astype(BF16)
        out_ref[part * 16 : part * 16 + 16, 2048:] = rounded
        x = x - rounded.astype(F32)


def head_kernel(teacher_ref, student_ref, student_gain_ref, out_ref, squares_ref):
    student_f = student_ref[...].astype(F32)
    mean = jnp.sum(student_f * student_f, axis=1, keepdims=True) / 2048
    out_ref[:, :2048] = (student_f * lax.rsqrt(mean + EPS) * student_gain_ref[...]).astype(BF16)
    out_ref[:, 2048:] = jnp.zeros((128, 128), BF16)
    squares = []
    for i in range(16):
        t = teacher_ref[i * 128 : (i + 1) * 128, :].astype(F32)
        t = t * t
        t = t[:, :128] + t[:, 128:256] + t[:, 256:384] + t[:, 384:]
        squares.append(jnp.sum(t.T, axis=0, keepdims=True))
    squares = jnp.concatenate(squares, axis=0)
    squares_ref[...] = squares
    put_parts(out_ref, squares)


def join_kernel(rows_ref, cross_ref, out_ref, buffer, sem):
    buffer[...] = rows_ref[...]
    squares = cross_ref[...]
    for part in (2, 1, 0):
        squares += rows_ref[part * 16 : part * 16 + 16, 2048:].astype(F32)
    put_parts(buffer, squares)
    copy = pltpu.make_async_copy(buffer, out_ref, sem)
    copy.start()
    copy.wait()


def place_kernel(z_ref, *rest):
    shards, (proj_ref, count_ref) = rest[:9], rest[9:]
    z = z_ref[0]
    tails = jnp.zeros((16, 512), F32)
    for offset, shard in zip((0, 1, 2, 3, -1, -2, -3), shards):
        at = lax.rem(z + (offset + 8), 8) * 128
        for x in range(2):
            proj_ref[pl.ds(pl.multiple_of(x * 1024 + at, 128), 128), :] = shard[x * 128 : (x + 1) * 128, :]
        tails += shard[256:272, :].astype(F32)
    at = lax.rem(z + 4, 8) * 128
    proj_ref[pl.ds(pl.multiple_of(at, 128), 128), :] = shards[7][...]
    proj_ref[pl.ds(pl.multiple_of(1024 + at, 128), 128), :] = shards[8][:128, :]
    tails += shards[8][128:144, :].astype(F32)
    lane = lax.broadcasted_iota(jnp.int32, (16, 512), 1)
    weight = jnp.where(lane == 0, 4.0, jnp.where(lane == 1, 0.25, 0.0))
    count_ref[...] = jnp.full((8, 128), jnp.sum(tails * weight), F32)


def load_rows(rows_hbm, rows, sems):
    copies = [
        pltpu.make_async_copy(rows_hbm.at[pl.ds(i * 4, 4)], rows.at[pl.ds(i * 4, 4)], sems.at[i]) for i in range(2)
    ]
    for copy in copies:
        copy.start()
    return copies


def slopes(i, half, length, factor, rows, proj_ref, teacher_ref, scale, gain):
    predicted = jnp.dot(rows, proj_ref[...], preferred_element_type=F32)
    lane = lax.broadcasted_iota(jnp.int32, (128, 128), 1)
    row = lax.broadcasted_iota(jnp.int32, (128, 1), 0)
    loss = jnp.zeros((8, 512), F32)
    found = []
    for b in range(4):
        place = (i * 4 + b) * 2 + half
        s = jnp.sum(jnp.where(lane == place, scale, 0.0), axis=1, keepdims=True)
        target = teacher_ref[i * 4 + b, half].astype(F32) * s * gain
        valid = (place * 128 + row) < length
        diff = jnp.where(valid, predicted[b * 128 : (b + 1) * 128] - target, 0.0)
        found.append((diff * factor).astype(BF16))
        loss += jnp.sum((diff * diff).reshape(16, 8, 512), axis=0)
    loss = loss[:, :128] + loss[:, 128:256] + loss[:, 256:384] + loss[:, 384:]
    return jnp.concatenate(found, axis=0), loss


def grad_part(rows, slope, x):
    return lax.dot_general(
        rows[:, x * 1024 : (x + 1) * 1024], slope, (((0,), (0,)), ((), ())), preferred_element_type=F32
    )


def columns(scale):
    return jnp.concatenate([scale, jnp.zeros((112, 128), F32)], axis=0).T


def near_kernel(ints, rows_hbm, proj_ref, count_ref, teacher_ref, gain_ref, *rest):
    grad_ref, loss_ref, scale_ref, proj_out, rows_ref, notes, sems = rest
    notes_copy = pltpu.make_async_copy(rows_hbm.at[:, pl.ds(0, 48), pl.ds(2048, 128)], notes, sems.at[2])
    notes_copy.start()
    copies = load_rows(rows_hbm, rows_ref, sems)
    proj_out[...] = proj_ref[...]
    notes_copy.wait()
    squares = jnp.zeros((16, 128), F32)
    for part in (2, 1, 0):
        for y in range(8):
            squares += notes[y, part * 16 : part * 16 + 16, :].astype(F32)
    scale = lax.rsqrt(squares / TW + EPS)
    scale_ref[...] = scale
    scale = columns(scale)
    factor = 2.0 / count_ref[0:1, 0:1]
    for i in range(2):
        copies[i].wait()
        rows = rows_ref[i * 4 : i * 4 + 4, :, :2048].reshape(512, 2048)
        slope, loss = slopes(i, ints[0], ints[1], factor, rows, proj_ref, teacher_ref, scale, gain_ref[...])
        loss_ref[...] = loss if i == 0 else loss_ref[...] + loss
        for x in range(2):
            lanes = slice(x * 512, (x + 1) * 512)
            part = grad_part(rows, slope, x)
            grad_ref[:, lanes] = part if i == 0 else grad_ref[:, lanes] + part


def far_kernel(ints, rows_hbm, proj_ref, count_ref, teacher_ref, gain_ref, *rest):
    scale_ref, grad_in, loss_in, grad_ref, sums_ref, rows_ref, sems = rest
    copies = load_rows(rows_hbm, rows_ref, sems)
    scale = columns(scale_ref[...])
    factor = 2.0 / count_ref[0:1, 0:1]
    sums_ref[16:24, :] = loss_in[...]
    for i in range(2):
        copies[i].wait()
        rows = rows_ref[i * 4 : i * 4 + 4, :, :2048].reshape(512, 2048)
        slope, loss = slopes(i, 1 - ints[0], ints[1], factor, rows, proj_ref, teacher_ref, scale, gain_ref[...])
        sums_ref[16:24, :] += loss
        for x in range(2):
            lanes = slice(x * 512, (x + 1) * 512)
            part = grad_part(rows, slope, x)
            grad_ref[:, lanes] = (grad_in[:, lanes] if i == 0 else grad_ref[:, lanes]) + part
    for x in range(2):
        g = grad_ref[:, x * 512 : (x + 1) * 512] * proj_ref[x * 1024 : (x + 1) * 1024, :].astype(F32)
        g = g[:, :128] + g[:, 128:256] + g[:, 256:384] + g[:, 384:]
        sums_ref[x * 8 : (x + 1) * 8, :] = jnp.sum(g.reshape(8, 128, 128), axis=2)


def own_rows(projection, teacher_gain, lengths):
    length = lengths[0]
    lane = lax.broadcasted_iota(jnp.int32, (8, 512), 1)
    digits = jnp.where(lane == 0, length >> 4, jnp.where(lane == 1, length & 15, 0)).astype(BF16)
    return jnp.concatenate([projection, digits, jnp.broadcast_to(teacher_gain, (8, 512))], axis=0)


def projection_flips(own):
    return [
        lax.ppermute(own, ("xl", "xh"), [(i, i ^ (fx * 2 + fc)) for i in range(4)]) for fx, fc in ((0, 1), (1, 0), (1, 1))
    ]


def projection_block(own, by_xh, by_xl, by_both):
    xl, xh = lax.axis_index("xl"), lax.axis_index("xh")
    parts = []
    for x in (0, 1):
        for k in (0, 1):
            a = jnp.where(xh == k, own, by_xh)
            b = jnp.where(xh == k, by_xl, by_both)
            parts.append(jnp.where(xl == x, a, b))
    return jnp.concatenate([p[:64] for p in parts] + [p[64:68] for p in parts], axis=0)


def on_device(teacher_hidden, teacher_gain, student_hidden, student_gain, projection, lengths):
    c, xl, xh, z = (lax.axis_index(a) for a in ("c", "xl", "xh", "z"))
    own = lax.ppermute(own_rows(projection, teacher_gain, lengths), ("c", "xh"), SWAP)
    scaled, squares = call(
        head_kernel,
        "head",
        [VMEM] * 3,
        [VMEM] * 2,
        [((128, WIDE), BF16), ((16, 128), F32)],
        [],
        10**7,
        teacher_hidden,
        student_hidden,
        student_gain.reshape(1, 2048),
    )
    scaled, squares, own = tie(scaled, squares, own)
    scaled = lax.ppermute(scaled, ("c", "xh"), SWAP)
    cross = lax.ppermute(squares, ("c", "xh"), CROSS)
    flips = projection_flips(own)
    scaled, cross, flips[0] = tie(scaled, cross, flips[0])
    (joined,) = call(
        join_kernel,
        "join",
        [VMEM] * 2,
        [HBM],
        [((128, WIDE), BF16)],
        [pltpu.VMEM((128, WIDE), BF16), pltpu.SemaphoreType.DMA],
        10**5,
        scaled,
        cross,
    )
    near = lax.all_gather(joined, "y", axis=0, tiled=True)

    block = projection_block(own, *flips)
    up1, down1 = shift(block, "z", 8, 1), shift(block, "z", 8, -1)
    teacher, _ = tie(teacher_hidden, block)
    teacher = lax.ppermute(teacher, ("c", "xh"), SWAP)
    up2, down2 = shift(up1, "z", 8, 1), shift(down1, "z", 8, -1)
    up3, down3 = shift(up2, "z", 8, 1), shift(down2, "z", 8, -1)
    up3, down3, teacher = tie(up3, down3, teacher)
    teacher = teacher.reshape(8, 2, 128, 512)
    down4 = shift(down3[:128], "z", 8, -1)
    up4 = shift(up3[128:], "z", 8, 1)
    proj_full, count = call(
        place_kernel,
        "place",
        [SMEM] + [VMEM] * 9,
        [VMEM] * 2,
        [((2048, 512), BF16), ((8, 128), F32)],
        [],
        10**6,
        z.reshape(1),
        *(block, down1, down2, down3, up1, up2, up3, down4, up4),
    )
    gain = own[72:73].astype(F32)
    length = (own[64, 0].astype(F32) * 16 + own[64, 1].astype(F32)).astype(jnp.int32)
    ints = jnp.stack([c, length]).astype(jnp.int32)
    near, proj_full, ints, gain = tie(near, proj_full, ints, gain)
    far = flip(near, "c", 2, 1)
    grad, loss_part, scale, proj_full = call(
        near_kernel,
        "near_rows",
        [SMEM, HBM] + [VMEM] * 4,
        [VMEM] * 4,
        [((1024, 1024), F32), ((8, 128), F32), ((16, 128), F32), ((2048, 512), BF16)],
        [pltpu.VMEM((8, 128, WIDE), BF16), pltpu.VMEM((8, 48, 128), BF16), pltpu.SemaphoreType.DMA((3,))],
        4 * 1024 * 2048 * 512,
        *(ints, near.reshape(8, 128, WIDE), proj_full, count, teacher, gain),
    )
    grad, sums = call(
        far_kernel,
        "far_rows",
        [SMEM, HBM] + [VMEM] * 7,
        [VMEM] * 2,
        [((1024, 1024), F32), ((24, 128), F32)],
        [pltpu.VMEM((8, 128, WIDE), BF16), pltpu.SemaphoreType.DMA((2,))],
        4 * 1024 * 2048 * 512,
        *(ints, far.reshape(8, 128, WIDE), proj_full, count, teacher, gain, scale, grad, loss_part),
    )
    mine = lax.psum_scatter(grad, "z", scatter_dimension=0, tiled=True)

    for axis, size, bit in (
        ("c", 2, 1),
        ("z", 8, 1),
        ("z", 8, 2),
        ("z", 8, 4),
        ("y", 8, 1),
        ("y", 8, 2),
        ("y", 8, 4),
        ("xl", 2, 1),
        ("xh", 2, 1),
    ):
        sums = sums + flip(sums, axis, size, bit)
    mine, sums = tie(mine, sums)
    rows = jnp.zeros((128, 512), F32)
    for fx in (0, 1):
        sent = lax.dynamic_slice(mine, (0, (xl ^ fx) * 512), (128, 512))
        rows += lax.ppermute(sent, ("xl", "c", "xh"), across(fx))
    sent = lax.dynamic_slice(rows, ((1 - c) * 64, 0), (64, 512))
    grad_proj = lax.dynamic_slice(rows, (c * 64, 0), (64, 512)) + flip(sent, "c", 2, 1)
    loss = jnp.sum(sums[16:]) / (count[0, 0] * TW)
    grad_gain = sums[:16].reshape(2048) / student_gain
    return (loss, grad_gain, grad_proj)


def solution(mesh):
    parts = Mesh(mesh.devices.reshape(2, 8, 2, 8, 2), DP + TENSOR)
    return jax.shard_map(
        on_device,
        mesh=parts,
        in_specs=(P(DP, TENSOR), P(TENSOR), P(DP + TENSOR, None), P(), P(DP, TENSOR), P(DP)),
        out_specs=(P(), P(), P(DP, TENSOR)),
        check_vma=False,
    )
```

```python
import jax
import jax.numpy as jnp
from jax import lax
from jax.experimental import pallas as pl
from jax.experimental.pallas import tpu as pltpu
from jax.sharding import Mesh, PartitionSpec as P

TW = 8192
EPS = 1e-06
WIDE = 2176
F32, BF16 = jnp.float32, jnp.bfloat16
DP = ("xl", "z", "c")
TENSOR = ("y", "xh")


SWAP = [(0, 0), (1, 2), (2, 1), (3, 3)]


CROSS = [(c * 2 + xh, (1 - xh) * 2 + c) for c in (0, 1) for xh in (0, 1)]
VMEM = pl.BlockSpec(memory_space=pltpu.VMEM)
SMEM = pl.BlockSpec(memory_space=pltpu.SMEM)
HBM = pl.BlockSpec(memory_space=pltpu.HBM)


def flip(x, axis, size, bit):
    return lax.ppermute(x, axis, [(i, i ^ bit) for i in range(size)])


def shift(x, axis, size, by):
    return lax.ppermute(x, axis, [(i, (i + by) % size) for i in range(size)])


def across(flip_xl):
    return [
        (xl * 4 + c * 2 + xh, (xl ^ flip_xl) * 4 + xh * 2 + c) for xl in (0, 1) for c in (0, 1) for xh in (0, 1)
    ]


def tie(*arrays):
    return lax.optimization_barrier(arrays)


def call(kernel, name, in_specs, out_specs, outs, scratch, flops, *args):
    return pl.pallas_call(
        kernel,
        in_specs=in_specs,
        out_specs=out_specs,
        out_shape=[jax.ShapeDtypeStruct(shape, dtype) for shape, dtype in outs],
        scratch_shapes=scratch,
        compiler_params=pltpu.CompilerParams(vmem_limit_bytes=16 * 2**20),
        cost_estimate=pl.CostEstimate(flops=flops, bytes_accessed=6 * 2**20, transcendentals=0),
        name=name,
    )(*args)


def put_parts(out_ref, x):
    for part in range(3):
        rounded = x.astype(BF16)
        out_ref[part * 16 : part * 16 + 16, 2048:] = rounded
        x = x - rounded.astype(F32)


def head_kernel(teacher_ref, student_ref, student_gain_ref, out_ref, squares_ref):
    student_f = student_ref[...].astype(F32)
    mean = jnp.sum(student_f * student_f, axis=1, keepdims=True) / 2048
    out_ref[:, :2048] = (student_f * lax.rsqrt(mean + EPS) * student_gain_ref[...]).astype(BF16)
    out_ref[:, 2048:] = jnp.zeros((128, 128), BF16)
    squares = []
    for i in range(16):
        t = teacher_ref[i * 128 : (i + 1) * 128, :].astype(F32)
        t = t * t
        t = t[:, :128] + t[:, 128:256] + t[:, 256:384] + t[:, 384:]
        squares.append(jnp.sum(t.T, axis=0, keepdims=True))
    squares = jnp.concatenate(squares, axis=0)
    squares_ref[...] = squares
    put_parts(out_ref, squares)


def join_kernel(rows_ref, cross_ref, out_ref, buffer, sem):
    buffer[...] = rows_ref[...]
    squares = cross_ref[...]
    for part in (2, 1, 0):
        squares += rows_ref[part * 16 : part * 16 + 16, 2048:].astype(F32)
    put_parts(buffer, squares)
    copy = pltpu.make_async_copy(buffer, out_ref, sem)
    copy.start()
    copy.wait()


def place_kernel(z_ref, *rest):
    shards, (proj_ref, count_ref) = rest[:9], rest[9:]
    z = z_ref[0]
    tails = jnp.zeros((16, 512), F32)
    for offset, shard in zip((0, 1, 2, 3, -1, -2, -3), shards):
        at = lax.rem(z + (offset + 8), 8) * 128
        for x in range(2):
            proj_ref[pl.ds(pl.multiple_of(x * 1024 + at, 128), 128), :] = shard[x * 128 : (x + 1) * 128, :]
        tails += shard[256:272, :].astype(F32)
    at = lax.rem(z + 4, 8) * 128
    proj_ref[pl.ds(pl.multiple_of(at, 128), 128), :] = shards[7][...]
    proj_ref[pl.ds(pl.multiple_of(1024 + at, 128), 128), :] = shards[8][:128, :]
    tails += shards[8][128:144, :].astype(F32)
    lane = lax.broadcasted_iota(jnp.int32, (16, 512), 1)
    weight = jnp.where(lane == 0, 4.0, jnp.where(lane == 1, 0.25, 0.0))
    count_ref[...] = jnp.full((8, 128), jnp.sum(tails * weight), F32)


def load_rows(rows_hbm, rows, sems):
    copies = [
        pltpu.make_async_copy(rows_hbm.at[pl.ds(i * 4, 4)], rows.at[pl.ds(i * 4, 4)], sems.at[i]) for i in range(2)
    ]
    for copy in copies:
        copy.start()
    return copies


def slopes(i, half, length, factor, rows, proj_ref, teacher_ref, scale, gain):
    predicted = jnp.dot(rows, proj_ref[...], preferred_element_type=F32)
    lane = lax.broadcasted_iota(jnp.int32, (128, 128), 1)
    row = lax.broadcasted_iota(jnp.int32, (128, 1), 0)
    loss = jnp.zeros((8, 512), F32)
    found = []
    for b in range(4):
        place = (i * 4 + b) * 2 + half
        s = jnp.sum(jnp.where(lane == place, scale, 0.0), axis=1, keepdims=True)
        target = teacher_ref[i * 4 + b, half].astype(F32) * s * gain
        valid = (place * 128 + row) < length
        diff = jnp.where(valid, predicted[b * 128 : (b + 1) * 128] - target, 0.0)
        found.append((diff * factor).astype(BF16))
        loss += jnp.sum((diff * diff).reshape(16, 8, 512), axis=0)
    loss = loss[:, :128] + loss[:, 128:256] + loss[:, 256:384] + loss[:, 384:]
    return jnp.concatenate(found, axis=0), loss


def grad_part(rows, slope, x):
    return lax.dot_general(
        rows[:, x * 1024 : (x + 1) * 1024], slope, (((0,), (0,)), ((), ())), preferred_element_type=F32
    )


def columns(scale):
    return jnp.concatenate([scale, jnp.zeros((112, 128), F32)], axis=0).T


def near_kernel(ints, rows_hbm, proj_ref, count_ref, teacher_ref, gain_ref, *rest):
    grad_ref, loss_ref, scale_ref, proj_out, rows_ref, notes, sems = rest
    notes_copy = pltpu.make_async_copy(rows_hbm.at[:, pl.ds(0, 48), pl.ds(2048, 128)], notes, sems.at[2])
    notes_copy.start()
    copies = load_rows(rows_hbm, rows_ref, sems)
    proj_out[...] = proj_ref[...]
    notes_copy.wait()
    squares = jnp.zeros((16, 128), F32)
    for part in (2, 1, 0):
        for y in range(8):
            squares += notes[y, part * 16 : part * 16 + 16, :].astype(F32)
    scale = lax.rsqrt(squares / TW + EPS)
    scale_ref[...] = scale
    scale = columns(scale)
    factor = 2.0 / count_ref[0:1, 0:1]
    for i in range(2):
        copies[i].wait()
        rows = rows_ref[i * 4 : i * 4 + 4, :, :2048].reshape(512, 2048)
        slope, loss = slopes(i, ints[0], ints[1], factor, rows, proj_ref, teacher_ref, scale, gain_ref[...])
        loss_ref[...] = loss if i == 0 else loss_ref[...] + loss
        for x in range(2):
            lanes = slice(x * 512, (x + 1) * 512)
            part = grad_part(rows, slope, x)
            grad_ref[:, lanes] = part if i == 0 else grad_ref[:, lanes] + part


def far_kernel(ints, rows_hbm, proj_ref, count_ref, teacher_ref, gain_ref, *rest):
    scale_ref, grad_in, loss_in, grad_ref, sums_ref, rows_ref, sems = rest
    copies = load_rows(rows_hbm, rows_ref, sems)
    scale = columns(scale_ref[...])
    factor = 2.0 / count_ref[0:1, 0:1]
    sums_ref[16:24, :] = loss_in[...]
    for i in range(2):
        copies[i].wait()
        rows = rows_ref[i * 4 : i * 4 + 4, :, :2048].reshape(512, 2048)
        slope, loss = slopes(i, 1 - ints[0], ints[1], factor, rows, proj_ref, teacher_ref, scale, gain_ref[...])
        sums_ref[16:24, :] += loss
        for x in range(2):
            lanes = slice(x * 512, (x + 1) * 512)
            part = grad_part(rows, slope, x)
            grad_ref[:, lanes] = (grad_in[:, lanes] if i == 0 else grad_ref[:, lanes]) + part
    for x in range(2):
        g = grad_ref[:, x * 512 : (x + 1) * 512] * proj_ref[x * 1024 : (x + 1) * 1024, :].astype(F32)
        g = g[:, :128] + g[:, 128:256] + g[:, 256:384] + g[:, 384:]
        sums_ref[x * 8 : (x + 1) * 8, :] = jnp.sum(g.reshape(8, 128, 128), axis=2)


def own_rows(projection, teacher_gain, lengths):
    length = lengths[0]
    lane = lax.broadcasted_iota(jnp.int32, (8, 512), 1)
    digits = jnp.where(lane == 0, length >> 4, jnp.where(lane == 1, length & 15, 0)).astype(BF16)
    return jnp.concatenate([projection, digits, jnp.broadcast_to(teacher_gain, (8, 512))], axis=0)


def projection_flips(own):
    return [
        lax.ppermute(own, ("xl", "xh"), [(i, i ^ (fx * 2 + fc)) for i in range(4)]) for fx, fc in ((0, 1), (1, 0), (1, 1))
    ]


def projection_block(own, by_xh, by_xl, by_both):
    xl, xh = lax.axis_index("xl"), lax.axis_index("xh")
    parts = []
    for x in (0, 1):
        for k in (0, 1):
            a = jnp.where(xh == k, own, by_xh)
            b = jnp.where(xh == k, by_xl, by_both)
            parts.append(jnp.where(xl == x, a, b))
    return jnp.concatenate([p[:64] for p in parts] + [p[64:68] for p in parts], axis=0)


def on_device(teacher_hidden, teacher_gain, student_hidden, student_gain, projection, lengths):
    c, xl, xh, z = (lax.axis_index(a) for a in ("c", "xl", "xh", "z"))
    own = lax.ppermute(own_rows(projection, teacher_gain, lengths), ("c", "xh"), SWAP)
    scaled, squares = call(
        head_kernel,
        "head",
        [VMEM] * 3,
        [VMEM] * 2,
        [((128, WIDE), BF16), ((16, 128), F32)],
        [],
        10**7,
        teacher_hidden,
        student_hidden,
        student_gain.reshape(1, 2048),
    )
    scaled, squares, own = tie(scaled, squares, own)
    scaled = lax.ppermute(scaled, ("c", "xh"), SWAP)
    cross = lax.ppermute(squares, ("c", "xh"), CROSS)
    flips = projection_flips(own)
    scaled, cross, flips[0], flips[1] = tie(scaled, cross, flips[0], flips[1])
    (joined,) = call(
        join_kernel,
        "join",
        [VMEM] * 2,
        [HBM],
        [((128, WIDE), BF16)],
        [pltpu.VMEM((128, WIDE), BF16), pltpu.SemaphoreType.DMA],
        10**5,
        scaled,
        cross,
    )
    near = lax.all_gather(joined, "y", axis=0, tiled=True)

    block = projection_block(own, *flips)
    up1, down1 = shift(block, "z", 8, 1), shift(block, "z", 8, -1)
    teacher, _ = tie(teacher_hidden, block)
    teacher = lax.ppermute(teacher, ("c", "xh"), SWAP)
    up2, down2 = shift(up1, "z", 8, 1), shift(down1, "z", 8, -1)
    up3, down3 = shift(up2, "z", 8, 1), shift(down2, "z", 8, -1)
    up3, down3, teacher = tie(up3, down3, teacher)
    teacher = teacher.reshape(8, 2, 128, 512)
    down4 = shift(down3[:128], "z", 8, -1)
    up4 = shift(up3[128:], "z", 8, 1)
    proj_full, count = call(
        place_kernel,
        "place",
        [SMEM] + [VMEM] * 9,
        [VMEM] * 2,
        [((2048, 512), BF16), ((8, 128), F32)],
        [],
        10**6,
        z.reshape(1),
        *(block, down1, down2, down3, up1, up2, up3, down4, up4),
    )
    gain = own[72:73].astype(F32)
    length = (own[64, 0].astype(F32) * 16 + own[64, 1].astype(F32)).astype(jnp.int32)
    ints = jnp.stack([c, length]).astype(jnp.int32)
    near, proj_full, ints, gain = tie(near, proj_full, ints, gain)
    far = flip(near, "c", 2, 1)
    grad, loss_part, scale, proj_full = call(
        near_kernel,
        "near_rows",
        [SMEM, HBM] + [VMEM] * 4,
        [VMEM] * 4,
        [((1024, 1024), F32), ((8, 128), F32), ((16, 128), F32), ((2048, 512), BF16)],
        [pltpu.VMEM((8, 128, WIDE), BF16), pltpu.VMEM((8, 48, 128), BF16), pltpu.SemaphoreType.DMA((3,))],
        4 * 1024 * 2048 * 512,
        *(ints, near.reshape(8, 128, WIDE), proj_full, count, teacher, gain),
    )
    grad, sums = call(
        far_kernel,
        "far_rows",
        [SMEM, HBM] + [VMEM] * 7,
        [VMEM] * 2,
        [((1024, 1024), F32), ((24, 128), F32)],
        [pltpu.VMEM((8, 128, WIDE), BF16), pltpu.SemaphoreType.DMA((2,))],
        4 * 1024 * 2048 * 512,
        *(ints, far.reshape(8, 128, WIDE), proj_full, count, teacher, gain, scale, grad, loss_part),
    )
    mine = lax.psum_scatter(grad, "z", scatter_dimension=0, tiled=True)

    for axis, size, bit in (
        ("c", 2, 1),
        ("z", 8, 1),
        ("z", 8, 2),
        ("z", 8, 4),
        ("y", 8, 1),
        ("y", 8, 2),
        ("y", 8, 4),
        ("xl", 2, 1),
        ("xh", 2, 1),
    ):
        sums = sums + flip(sums, axis, size, bit)
    mine, sums = tie(mine, sums)
    rows = jnp.zeros((128, 512), F32)
    for fx in (0, 1):
        sent = lax.dynamic_slice(mine, (0, (xl ^ fx) * 512), (128, 512))
        rows += lax.ppermute(sent, ("xl", "c", "xh"), across(fx))
    sent = lax.dynamic_slice(rows, ((1 - c) * 64, 0), (64, 512))
    grad_proj = lax.dynamic_slice(rows, (c * 64, 0), (64, 512)) + flip(sent, "c", 2, 1)
    loss = jnp.sum(sums[16:]) / (count[0, 0] * TW)
    grad_gain = sums[:16].reshape(2048) / student_gain
    return (loss, grad_gain, grad_proj)


def solution(mesh):
    parts = Mesh(mesh.devices.reshape(2, 8, 2, 8, 2), DP + TENSOR)
    return jax.shard_map(
        on_device,
        mesh=parts,
        in_specs=(P(DP, TENSOR), P(TENSOR), P(DP + TENSOR, None), P(), P(DP, TENSOR), P(DP)),
        out_specs=(P(), P(), P(DP, TENSOR)),
        check_vma=False,
    )
```
